32 devices in a mesh: row: 4 (over y, x), col: 8 (over z, core).
Axes of the slice: x: 2, y: 2, z: 4, core: 2. Of those that a mesh axis runs over, the one named last changes fastest.
Arguments:
- kernel: float32 [10240, 10240], P('row', 'col'), may hold values from 0 to 3, as said below
- noise: float32 [10240], P('row'), may hold values from 0.3 to 1
Outputs:
- factored: float32 [10240, 10240], P('row', 'col')
The draws below stay inside these ranges and needn't reach their ends.
Inputs may be any that keep to these rules, and one draw needn't show every extreme that they name: In global order kernel is symmetric and positive semidefinite, and all its entries are positive.
All inputs are finite; a program needn't handle non-finite values.
Results may differ from the reference program's by a relative error of at most 0.0001.
Values sent between devices are 32-bit elements; how exact they have to be, the bound alone decides.
No kernel may reach another device: no remote copies, remote signals or barrier semaphores. Data moves between devices by JAX's collectives and lax.ppermute only.
A program may use at most 128 MiB of HBM per device.

```python
import math
import jax
import jax.numpy as jnp
from jax import lax

NB = 256
KB = 5
RB = 10
ORDER = 10240
N_ROW = 4
N_COL = 8


def point_index(stored, per_group, groups):
    span = per_group * NB
    group = stored // span
    inner = stored % span
    return (inner // NB * groups + group) * NB + stored % NB


def draw_kernel(key, part):
    key = jax.random.fold_in(key, 7)
    coord_key, scale_key = jax.random.split(key)
    coords = jax.random.uniform(coord_key, (4, ORDER), jnp.float32)
    scales = jnp.exp(jax.random.uniform(scale_key, (ORDER,), jnp.float32, math.log(0.75), math.log(1.33)))
    stored = jnp.arange(ORDER, dtype=jnp.int32)
    row_points = point_index(stored, RB, N_ROW)
    col_points = point_index(stored, KB, N_COL)
    distance = jnp.zeros((ORDER, ORDER), jnp.float32)
    for axis_number in range(4):
        line = coords[axis_number]
        distance = distance + jnp.abs(line[row_points][:, None] - line[col_points][None, :])
    values = scales[row_points][:, None] * scales[col_points][None, :] * jnp.exp(-distance)
    return values.astype(jnp.float32)


def steps_of(stream_key, shape, shards, smallest, top_value):
    loudness, own = 1.0, jax.random.fold_in(stream_key, 6)
    for dim, blocks in shards:
        heights = jnp.exp(jax.random.uniform(jax.random.fold_in(own, dim), (blocks,), jnp.float32, smallest / len(shards), top_value / len(shards)))
        loudness = loudness * jnp.repeat(heights, shape[dim] // blocks).reshape([-1 if axis == dim else 1 for axis in range(len(shape))])
    return loudness


def setup_inputs(seed: int = 0) -> dict:
    key_list = jax.random.split(jax.random.key(seed), 3)
    kernel = draw_kernel(jax.random.fold_in(key_list[2], 71), 0)
    noise = jnp.clip(0.3 + 0.7 * jax.random.uniform(key_list[1], (ORDER,), jnp.float32) ** steps_of(key_list[1], (ORDER,), ((0, 4),), -0.2, 0.2), 0.3, 1.0)
    return dict(kernel=kernel, noise=noise)


def rows_global(x, parts):
    total = x.shape[0]
    per = total // NB // parts
    return x.reshape(parts, per, NB, x.shape[1]).transpose(1, 0, 2, 3).reshape(total, x.shape[1])

def rows_stored(x, parts):
    total = x.shape[0]
    per = total // NB // parts
    return x.reshape(per, parts, NB, x.shape[1]).transpose(1, 0, 2, 3).reshape(total, x.shape[1])

def factor_block(block):
    whole = jnp.tril(block) + jnp.tril(block, -1).T
    factor = jnp.linalg.cholesky(whole)
    eye = jnp.eye(block.shape[0], dtype=block.dtype)
    inverse = lax.linalg.triangular_solve(factor, eye, left_side=True, lower=True)
    return (factor, inverse)

def reference(kernel, noise):
    matrix = rows_global(kernel, N_ROW)
    matrix = rows_global(matrix.T, N_COL).T
    diag_noise = rows_global(noise[:, None], N_ROW)[:, 0]
    index = jnp.arange(ORDER)
    matrix = matrix.at[index, index].add(diag_noise)
    block_id = index // NB
    for k in range(2):
        low = k * NB
        high = low + NB
        factor, inverse = factor_block(matrix[low:high, low:high])
        panel = jnp.dot(matrix[high:, low:high].astype(jnp.float32), inverse.T.astype(jnp.float32), precision=lax.Precision.HIGHEST, preferred_element_type=jnp.float32)
        update = jnp.dot(panel.astype(jnp.float32), panel.T.astype(jnp.float32), precision=lax.Precision.HIGHEST, preferred_element_type=jnp.float32)
        rest = block_id[high:]
        keep = rest[:, None] >= rest[None, :]
        trailing = jnp.where(keep, matrix[high:, high:] - update, matrix[high:, high:])
        matrix = matrix.at[high:, high:].set(trailing)
        matrix = matrix.at[high:, low:high].set(panel)
        matrix = matrix.at[low:high, low:high].set(factor)
    matrix = rows_stored(matrix.T, N_COL).T
    return rows_stored(matrix, N_ROW)
```

```python
import functools
import jax
import jax.numpy as jnp
from jax import lax
from jax.sharding import PartitionSpec as P
from jax.experimental import pallas as pl
from jax.experimental.pallas import tpu as pltpu

NB = 256
HB = 128
HIGHEST = lax.Precision.HIGHEST


def dot_nt(a, b):
    return lax.dot_general(
        a, b, (((1,), (1,)), ((), ())), precision=HIGHEST, preferred_element_type=jnp.float32
    )


def dot_nn(a, b):
    return jnp.dot(a, b, precision=HIGHEST, preferred_element_type=jnp.float32)


def half_factor(work, unit, upper, lower_inv, spread):
    groups = HB // 8
    for b in range(groups):
        r0 = 8 * b
        cols = []
        for c in range(8):
            col = [
                jnp.broadcast_to(work[8 * g : 8 * g + 8, r0 + c : r0 + c + 1], (8, HB))
                for g in range(b, groups)
            ]
            spread[8 * c : 8 * c + 8, :] = col[0]
            cols.append(col)
        s = {}
        for c in range(8):
            for r in range(c, 8):
                s[r, c] = jnp.broadcast_to(spread[8 * c + r : 8 * c + r + 1, :], (8, HB))
        rows = [jnp.broadcast_to(work[r0 + r : r0 + r + 1, :], (8, HB)) for r in range(8)]
        unit_rows = [jnp.broadcast_to(unit[r0 + r : r0 + r + 1, :], (8, HB)) for r in range(8)]
        for k in range(8):
            scale = lax.rsqrt(s[k, k])
            for r in range(k + 1, 8):
                s[r, k] = s[r, k] * scale
            rows[k] = rows[k] * scale
            unit_rows[k] = unit_rows[k] * scale
            for g in range(1, groups - b):
                cols[k][g] = cols[k][g] * scale
            for c in range(k + 1, 8):
                for r in range(c, 8):
                    s[r, c] = s[r, c] - s[r, k] * s[c, k]
                rows[c] = rows[c] - s[c, k] * rows[k]
                unit_rows[c] = unit_rows[c] - s[c, k] * unit_rows[k]
                for g in range(1, groups - b):
                    cols[c][g] = cols[c][g] - s[c, k] * cols[k][g]
        for g in range(1, groups - b):
            at = slice(r0 + 8 * g, r0 + 8 * g + 8)
            take = [cols[k][g] * rows[k] for k in range(8)]
            work[at, :] = work[at, :] - (
                ((take[0] + take[1]) + (take[2] + take[3]))
                + ((take[4] + take[5]) + (take[6] + take[7]))
            )
            take = [cols[k][g] * unit_rows[k] for k in range(8)]
            unit[at, :] = unit[at, :] - (
                ((take[0] + take[1]) + (take[2] + take[3]))
                + ((take[4] + take[5]) + (take[6] + take[7]))
            )
        for k in range(8):
            upper[r0 + k : r0 + k + 1, :] = rows[k][:1]
            lower_inv[r0 + k : r0 + k + 1, :] = unit_rows[k][:1]


def first_half(block, work, unit, upper, lower_inv, spread, outs):
    factor, inverse, below, rest = outs
    row = lax.broadcasted_iota(jnp.int32, (HB, HB), 0)
    col = lax.broadcasted_iota(jnp.int32, (HB, HB), 1)
    work[...] = block[0]
    unit[...] = jnp.where(row == col, 1.0, 0.0)
    half_factor(work, unit, upper, lower_inv, spread)
    factor[...] = jnp.where(row >= col, upper[...].T, 0.0)
    inverse[...] = lower_inv[...]
    strip = dot_nt(block[1], lower_inv[...])
    below[...] = strip
    rest[...] = block[2] - dot_nt(strip, strip)


def start_kernel(block, factor, inverse, below, rest, work, unit, upper, lower_inv, spread):
    first_half(block, work, unit, upper, lower_inv, spread, (factor, inverse, below, rest))


def next_kernel(
    side, turned, block, prior, cross, factor, inverse, below, rest, left, work, unit, upper, lower_inv, spread
):
    raw = jnp.concatenate(
        [
            jnp.concatenate([side[0], turned[1].T], axis=1),
            jnp.concatenate([side[1], side[2]], axis=1),
        ],
        axis=0,
    )
    solved = dot_nt(raw, prior[...])
    cross[...] = solved
    update = dot_nt(solved, solved)
    left[0] = block[0] - update[:HB, :HB]
    left[1] = block[1] - update[HB:, :HB]
    left[2] = block[2] - update[HB:, HB:]
    first_half(left, work, unit, upper, lower_inv, spread, (factor, inverse, below, rest))


def finish_kernel(
    factor, inverse, below, rest, whole_factor, whole_inverse, work, unit, upper, lower_inv, spread
):
    row = lax.broadcasted_iota(jnp.int32, (HB, HB), 0)
    col = lax.broadcasted_iota(jnp.int32, (HB, HB), 1)
    work[...] = rest[...]
    unit[...] = jnp.where(row == col, 1.0, 0.0)
    half_factor(work, unit, upper, lower_inv, spread)
    whole_factor[:HB, :HB] = factor[...]
    whole_factor[:HB, HB:] = jnp.zeros((HB, HB), jnp.float32)
    whole_factor[HB:, :HB] = below[...]
    whole_factor[HB:, HB:] = jnp.where(row >= col, upper[...].T, 0.0)
    whole_inverse[:HB, :HB] = inverse[...]
    whole_inverse[:HB, HB:] = jnp.zeros((HB, HB), jnp.float32)
    whole_inverse[HB:, :HB] = -dot_nn(lower_inv[...], dot_nn(below[...], inverse[...]))
    whole_inverse[HB:, HB:] = lower_inv[...]


def factor_call(fn, args, outs, extra=()):
    half = pltpu.VMEM((HB, HB), jnp.float32)
    return pl.pallas_call(
        fn,
        out_shape=[jax.ShapeDtypeStruct(s, jnp.float32) for s in outs],
        scratch_shapes=[
            *extra,
            half,
            half,
            half,
            half,
            pltpu.VMEM((64, HB), jnp.float32),
        ],
        compiler_params=pltpu.CompilerParams(vmem_limit_bytes=32 * 2**20),
        cost_estimate=pl.CostEstimate(flops=0, bytes_accessed=0, transcendentals=0),
    )(*args)


QUARTERS = [(HB, HB)] * 4


def split(x):
    high = x.astype(jnp.bfloat16)
    return high, (x - high.astype(jnp.float32)).astype(jnp.bfloat16)


def mul(a, b):
    return jnp.dot(a, b, preferred_element_type=jnp.float32)


def mul_nt(a, b):
    return lax.dot_general(a, b, (((1,), (1,)), ((), ())), preferred_element_type=jnp.float32)


def wide_left(x):
    high, low = split(x)
    return jnp.concatenate([high, high, low], axis=1)


def wide_right(x):
    high, low = split(x)
    return jnp.concatenate([high, low, high], axis=1)


def solve_both(first, second, first_inverse, cross, second_inverse):
    left = mul_nt(wide_left(first), first_inverse)
    right = mul_nt(wide_left(second - mul_nt(wide_left(left), cross)), second_inverse)
    return left, right


def update_kernel(n_row, n_col, step_of, count, given, *refs):
    (place, matrix, noise, own, twin, here, there) = refs[:7]
    (first_factor, first_inverse, cross, second_factor, second_inverse) = refs[7:12]
    refs = refs[12:]
    if given is None:
        mine, other, out, high, low = refs[:5]
        refs = refs[5:]
    else:
        high, low, _, out = refs[:4]
        refs = refs[4:]
    tiles, rows_wide, edge, in_sem, out_sem = refs
    p, q = place[0], place[2]
    col_count = matrix.shape[1] // NB

    def rows_at(r):
        start = step_of(r) * NB
        return pl.ds(start if isinstance(start, int) else pl.multiple_of(start, NB), NB)

    def fetch(r):
        return pltpu.make_async_copy(matrix.at[rows_at(r), :], tiles.at[r], in_sem.at[r])

    def leave(r):
        return pltpu.make_async_copy(tiles.at[r], out.at[rows_at(r), :], out_sem.at[r])

    for r in range(count):
        fetch(r).start()
    inverses = (
        wide_right(first_inverse[...]),
        wide_right(cross[...]),
        wide_right(second_inverse[...]),
    )
    if given is None:
        odd = place[1] == 1
        left, right = solve_both(
            jnp.where(odd, other[...], mine[...]), jnp.where(odd, mine[...], other[...]), *inverses
        )
        high[:NB], low[:NB] = split(left.T)
        high[NB:], low[NB:] = split(right.T)
    by_columns = jnp.where(place[5] == 1, here[...], there[...])
    by_core = jnp.where(place[6] == 0, twin[...], own[...])
    first = jnp.where(place[3] == 1, own[...], twin[...])
    second = jnp.where(place[4] == 1, by_columns, by_core)
    left, right = solve_both(first.reshape(-1, NB), second.reshape(-1, NB), *inverses)
    edge[...] = jnp.where(q == 0, left, right).reshape(edge.shape)
    left_high, left_low = split(left)
    right_high, right_low = split(right)
    rows_wide[:, :NB] = left_high
    rows_wide[:, NB : 2 * NB] = right_high
    rows_wide[:, 2 * NB : 3 * NB] = left_low
    rows_wide[:, 3 * NB :] = right_low
    row = lax.broadcasted_iota(jnp.int32, (NB, NB), 0)
    col = lax.broadcasted_iota(jnp.int32, (NB, NB), 1)

    def one(r, _):
        here = pl.ds(pl.multiple_of(r * NB, NB), NB)
        i = step_of(r) * n_row + p
        active = jnp.minimum(lax.div(i - q + n_col, n_col), col_count)
        fetch(r).wait()
        for blocks in range(1, col_count + 1):

            @pl.when(active == blocks)
            def _():
                both = rows_wide[here, : 2 * NB]
                wide = jnp.concatenate([both, both, rows_wide[here, 2 * NB :]], axis=1)
                for c in range(blocks):
                    at = slice(c * NB, c * NB + NB)
                    tall = jnp.concatenate([high[:, at], low[:, at], high[:, at]], axis=0)
                    tiles[r, :, at] = tiles[r, :, at] - mul(wide, tall)

                @pl.when(i == (blocks - 1) * n_col + q)
                def _():
                    tiles[r, :, at] += jnp.where(row == col, noise[step_of(r)], 0.0)

        @pl.when((q < 2) & (i > q))
        def _():
            tiles[r, :, :NB] = jnp.where((q == 0) & (i == 1), cross[...], edge[r])

        @pl.when((q < 2) & (i == q))
        def _():
            tiles[r, :, :NB] = jnp.where(q == 0, first_factor[...], second_factor[...])

        leave(r).start()
        return 0

    lax.fori_loop(0, count, one, 0)
    for r in range(count):
        leave(r).wait()


def update(place, step_of, count, matrix, noise, rows, factored, n_row, n_col, cols=None, done=None):
    cols_local = matrix.shape[1]
    whole = pl.BlockSpec(memory_space=pltpu.VMEM)
    anywhere = pl.BlockSpec(memory_space=pl.ANY)
    part = jax.ShapeDtypeStruct((2 * NB, cols_local), jnp.bfloat16)
    result = jax.ShapeDtypeStruct(matrix.shape, jnp.float32)
    extra = cols if done is None else (*done[1:], done[0])
    solved = count + (cols_local // NB if done is None else 0)
    flops = 2 * 3 * NB * NB * (solved * 3 * NB + count * cols_local)
    outs = pl.pallas_call(
        functools.partial(update_kernel, n_row, n_col, step_of, count, done),
        in_specs=[pl.BlockSpec(memory_space=pltpu.SMEM), anywhere]
        + [whole] * 10
        + ([whole, whole] if done is None else [whole, whole, anywhere]),
        out_specs=[anywhere, whole, whole] if done is None else anywhere,
        out_shape=[result, part, part] if done is None else result,
        scratch_shapes=[
            pltpu.VMEM((count, NB, cols_local), jnp.float32),
            pltpu.VMEM((count * NB, 4 * NB), jnp.bfloat16),
            pltpu.VMEM((count, NB, NB), jnp.float32),
            pltpu.SemaphoreType.DMA((count,)),
            pltpu.SemaphoreType.DMA((count,)),
        ],
        input_output_aliases={} if done is None else {14: 0},
        compiler_params=pltpu.CompilerParams(vmem_limit_bytes=40 * 2**20),
        cost_estimate=pl.CostEstimate(
            flops=flops, bytes_accessed=count * NB * cols_local * 8, transcendentals=0
        ),
    )(place, matrix, noise, *rows, *factored, *extra)
    return outs if done is None else (outs, *done[1:])


def start_factor(corner):
    return factor_call(start_kernel, [corner], QUARTERS)


def finish_factor(part, side, turned, next_corner, before_first=(), before_last=()):
    part = [after(part[0], *before_first), *part[1:]]
    first_factor, first_inverse = factor_call(finish_kernel, part, [(NB, NB)] * 2)
    cross, *part = factor_call(
        next_kernel,
        [side, turned, next_corner, first_inverse],
        [(NB, NB)] + QUARTERS,
        [pltpu.VMEM((3, HB, HB), jnp.float32)],
    )
    part = [after(part[0], *before_last), *part[1:]]
    second_factor, second_inverse = factor_call(finish_kernel, part, [(NB, NB)] * 2)
    return first_factor, first_inverse, cross, second_factor, second_inverse


def low_part(x):
    return jnp.stack([x[:HB, :HB], x[HB:, :HB], x[HB:, HB:]])


def after(x, *others):
    return lax.optimization_barrier((x, *others))[0]


def blocks_of(x):
    return x.reshape(-1, NB, NB)


def head_noise(noise):
    return jnp.where(jnp.arange(NB)[:, None] == jnp.arange(NB)[None, :], noise[:NB, None], 0.0)


def arrange(own, other, core):
    first = jnp.where(core == 0, own, other)
    second = jnp.where(core == 0, other, own)
    return first[0], first[1], second[0], second[1]


def body_general(kernel, noise):
    n_row = lax.axis_size("row")
    n_col = lax.axis_size("col")
    p = lax.axis_index("row")
    q = lax.axis_index("col")
    chunks = kernel.shape[0] // NB
    planes = n_col // 2
    plane = q // 2
    core = q % 2

    def twin(x):
        return lax.ppermute(x, "col", [(c, c ^ 1) for c in range(n_col)])

    mine = blocks_of(kernel[:, :NB])
    sent, other, got = [], [], None
    for s in range(chunks + planes - 1):
        now = mine[0] if s == 0 else got
        if 0 < s < chunks:
            now = jnp.where(plane == 0, mine[s], got)
        sent.append(now)
        other.append(twin(now))
        pairs = [
            (2 * z + c, 2 * z + 2 + c)
            for z in range(planes - 1)
            if 0 <= s - z < chunks
            for c in range(2)
        ]
        if pairs:
            got = lax.ppermute(now, "col", pairs)
    own = lax.dynamic_slice_in_dim(jnp.stack(sent), plane, chunks)
    other = lax.dynamic_slice_in_dim(jnp.stack(other), plane, chunks)

    block = own[0]
    block = low_part(jnp.where(p == core, block + head_noise(noise), block))
    swapped = lax.ppermute(block, "row", [(r, r ^ 1) for r in range(2)])
    even = p % 2 == 0
    strip = jnp.stack([jnp.where(even, block, swapped), jnp.where(even, swapped, block)])
    step = 2
    while step < n_row:
        more = lax.ppermute(strip, "row", [(r, r + step) for r in range(step)])
        strip = jnp.where(p >= step, more, strip)
        step *= 2
    corner, *rest = arrange(strip, twin(strip), core)
    factored = finish_factor(start_factor(corner), *rest)

    tops = lax.all_gather(kernel[:NB].T, "row")
    none = jnp.zeros_like(p)
    place = jnp.stack([p, none, q, 1 - core, none, none, core]).astype(jnp.int32)
    return update(
        place,
        lambda r: r,
        chunks,
        kernel,
        noise.reshape(-1, 1, NB),
        (own, other, own, own),
        factored,
        n_row,
        n_col,
        cols=(tops[0], tops[1]),
    )[0]


BOTH = ("row", "col")
N_COL = 8


def route(x, pairs):
    return lax.ppermute(x, BOTH, [(a[0] * N_COL + a[1], b[0] * N_COL + b[1]) for a, b in pairs])


def spread_inverses(factored, earlier, between, plane, core):
    _, first, cross, _, second = factored
    halves = (
        jnp.concatenate([low_part(first), jnp.stack([cross[:HB, :HB], cross[:HB, HB:]])]),
        jnp.concatenate([jnp.stack([cross[HB:, :HB], cross[HB:, HB:]]), low_part(second)]),
    )
    here = after(jnp.where(core == 0, halves[0], halves[1]), *earlier)
    z = route(here, [((r, c), (r, 4 + c)) for r in range(4) for c in (0, 1)])
    here = after(jnp.where(plane == 2, z, here), *between)
    z = route(here, [((r, k + c), (r, k + 2 + c)) for r in range(4) for k in (0, 4) for c in (0, 1)])
    here = jnp.where(plane % 2 == 1, z, here)
    other = route(here, TWINS)
    top = jnp.where(core == 0, here, other)
    low = jnp.where(core == 0, other, here)
    zero = jnp.zeros((HB, HB), jnp.float32)

    def square(a, b, c, d):
        return jnp.concatenate(
            [jnp.concatenate([a, b], axis=1), jnp.concatenate([c, d], axis=1)], axis=0
        )

    return (
        square(top[0], zero, top[1], top[2]),
        square(top[3], top[4], low[0], low[1]),
        square(low[2], zero, low[3], low[4]),
    )


TWINS = [((r, c), (r, c ^ 1)) for r in range(4) for c in range(N_COL)]


def body_four(kernel, noise):
    p = lax.axis_index("row")
    q = lax.axis_index("col")
    plane = q // 2
    core = q % 2
    home = core == p % 2
    low_line = p < 2
    n_cols = kernel.shape[1] // NB
    cut = (n_cols - 1) // 2
    early, late = slice(1, 1 + cut), slice(1 + cut, 1 + 2 * cut)

    strips = kernel.reshape(n_cols, 2, NB, -1)

    def even(part):
        return strips[part, 0, :, :NB]

    def odd(part):
        return strips[part, 1, :, :NB]

    blocks = blocks_of(kernel[:NB].T)
    middle = blocks[early]
    others = jnp.concatenate([blocks[:1], blocks[late]], axis=0)
    along_y = [((a, c), (a + 2, c)) for a in range(2) for c in range(N_COL)]
    along_x = [((a, c), (a ^ 1, c)) for a in range(4) for c in range(N_COL)]
    low, high = (0, 1), (2, 3)
    up = lambda z, lines: [((r, 2 * z + c), (r, 2 * z + 2 + c)) for r in lines for c in (0, 1)]
    lift = [((s, 4 + r), (r, 6 + s)) for r in low for s in (0, 1)]
    side = [((2 + s, r), (r, 4 + s)) for r in high for s in (0, 1)]
    corner = kernel[:NB, :NB]
    corner = low_part(jnp.where(p == core, corner + head_noise(noise), corner))

    got = route(corner, [((r, c), (r + 2, c)) for r in (0, 1) for c in (0, 1)])
    y1 = route(after(middle, got), along_y)
    h1 = route(jnp.where(plane == 0, even(early), middle), up(0, low) + lift)
    here = jnp.where(low_line, corner, got)
    lead_x = route(here, [((r, c), (r ^ 1, c)) for r in range(4) for c in (0, 1)])
    is_even = p % 2 == 0
    lead = jnp.stack([jnp.where(is_even, here, lead_x), jnp.where(is_even, lead_x, here)])
    lead_twin = route(lead, [((r, c), (r, c ^ 1)) for r in range(4) for c in (0, 1)])
    corner, *rest = arrange(lead, lead_twin, core)
    begun = start_factor(after(corner, h1))

    others = after(others, lead_x)
    y2 = route(others, along_y)
    mine1 = jnp.where(low_line, after(middle, lead_x), y1)
    x1 = route(after(mine1, begun[0]), along_x)

    h2 = route(
        jnp.where(
            plane == 0,
            even(late),
            jnp.where(plane == 1, jnp.where(low_line, h1, mine1), others[1:]),
        ),
        up(0, low) + up(1, low) + side + lift,
    )
    down = [((s, 4 + r), (r, 2 + s)) for r in low for s in (0, 1)]
    down += [((2 + s, 4 + r), (r, 4 + s)) for r in high for s in (0, 1)]
    d1 = route(after(mine1, begun[0]), down)
    e1 = route(odd(slice(0, n_cols)), up(0, high))
    factored = finish_factor(begun, *rest, before_last=(x1, h2, y2, d1, e1))
    mine2 = jnp.where(low_line, after(others, factored[2]), y2)
    x2 = route(after(mine2, x1), along_x)
    d2 = route(mine2, down)
    h2 = after(h2, factored[2])
    h3 = route(
        jnp.where((plane == 1) & ~low_line, mine2[1:], h2), up(1, low) + side + up(2, low + high)
    )
    h4 = route(h3, up(2, low + high))
    inverses = spread_inverses(factored, (h2,), (x2,), plane, core)
    factored = (factored[0], inverses[0], inverses[1], factored[3], inverses[2])

    given = lambda x, y: jnp.concatenate([y[:1], x, y[1:]], axis=0)
    col_mine = given(mine1, mine2)
    col_given = given(x1, x2)
    first_cols = jnp.where(is_even, col_mine, col_given)
    second_cols = jnp.where(is_even, col_given, col_mine)
    homes = [((r, c), (r, c ^ 1)) for r, c in [(0, 4), (1, 5), (2, 6), (3, 7), (2, 2), (3, 3)]]
    second_twin = route(second_cols, homes)

    by_odd = (low_line & (plane == 2)) | (~low_line & (plane == 3))
    by_even = ~low_line & (plane == 1)
    own_1 = jnp.where(
        by_odd,
        first_cols,
        jnp.where(
            plane == 0,
            odd(slice(0, n_cols)),
            jnp.where(
                by_even,
                e1,
                jnp.where(plane == 3, jnp.concatenate([h1[:1], h1, h2], axis=0), given(d1, d2)),
            ),
        ),
    )
    own_2 = jnp.where(
        plane == 0,
        even(slice(0, 1 + cut)),
        jnp.where(
            by_even,
            first_cols[: 1 + cut],
            given(jnp.where(plane == 1, h1, jnp.where(plane == 2, h2, h3)), h1[:1]),
        ),
    )

    def rows(own, part):
        return own, route(own, TWINS), second_cols[part], second_twin[part]

    def place(by):
        flags = [p, p % 2, q, jnp.where(by, home, core == 0), by, home, core]
        return jnp.stack([x.astype(jnp.int32) for x in flags])

    noise_rows = noise.reshape(-1, 1, NB)
    rows_1 = rows(own_1, slice(0, n_cols))
    rows_2 = rows(own_2, slice(0, 1 + cut))
    cols = (col_mine.reshape(-1, NB), col_given.reshape(-1, NB))
    done = update(
        place(by_odd),
        lambda r: 2 * r + 1,
        n_cols,
        kernel,
        noise_rows,
        rows_1,
        factored,
        4,
        N_COL,
        cols=cols,
    )
    h4 = after(h4, done[1])
    own_3 = jnp.where(
        plane == 0,
        even(late),
        jnp.where(
            by_even,
            first_cols[late],
            jnp.where(plane == 1, h2, jnp.where(plane == 2, h3, h4)),
        ),
    )
    rows_3 = rows(own_3, late)
    done = update(
        place(by_even), lambda r: 2 * r, 1 + cut, kernel, noise_rows, rows_2, factored, 4, N_COL, done=done
    )
    return update(
        place(by_even),
        lambda r: 2 * (1 + cut + r),
        cut,
        kernel,
        noise_rows,
        rows_3,
        factored,
        4,
        N_COL,
        done=done,
    )[0]


def body(kernel, noise):
    rows, cols = kernel.shape[0] // NB, kernel.shape[1] // NB
    mesh_of_four = lax.axis_size("row") == 4 and lax.axis_size("col") == N_COL
    if mesh_of_four and rows == 2 * cols and cols % 2 == 1 and cols > 2:
        return body_four(kernel, noise)
    return body_general(kernel, noise)


def solution(mesh):
    return jax.shard_map(
        body,
        mesh=mesh,
        in_specs=(P("row", "col"), P("row")),
        out_specs=P("row", "col"),
        check_vma=False,
    )
```

```python
import functools
import jax
import jax.numpy as jnp
from jax import lax
from jax.sharding import PartitionSpec as P
from jax.experimental import pallas as pl
from jax.experimental.pallas import tpu as pltpu

NB = 256
HB = 128
HIGHEST = lax.Precision.HIGHEST


def dot_nt(a, b):
    return lax.dot_general(
        a, b, (((1,), (1,)), ((), ())), precision=HIGHEST, preferred_element_type=jnp.float32
    )


def dot_nn(a, b):
    return jnp.dot(a, b, precision=HIGHEST, preferred_element_type=jnp.float32)


def half_factor(work, unit, upper, lower_inv, spread):
    groups = HB // 8
    for b in range(groups):
        r0 = 8 * b
        cols = []
        for c in range(8):
            col = [
                jnp.broadcast_to(work[8 * g : 8 * g + 8, r0 + c : r0 + c + 1], (8, HB))
                for g in range(b, groups)
            ]
            spread[8 * c : 8 * c + 8, :] = col[0]
            cols.append(col)
        s = {}
        for c in range(8):
            for r in range(c, 8):
                s[r, c] = jnp.broadcast_to(spread[8 * c + r : 8 * c + r + 1, :], (8, HB))
        rows = [jnp.broadcast_to(work[r0 + r : r0 + r + 1, :], (8, HB)) for r in range(8)]
        unit_rows = [jnp.broadcast_to(unit[r0 + r : r0 + r + 1, :], (8, HB)) for r in range(8)]
        for k in range(8):
            scale = lax.rsqrt(s[k, k])
            for r in range(k + 1, 8):
                s[r, k] = s[r, k] * scale
            rows[k] = rows[k] * scale
            unit_rows[k] = unit_rows[k] * scale
            for g in range(1, groups - b):
                cols[k][g] = cols[k][g] * scale
            for c in range(k + 1, 8):
                for r in range(c, 8):
                    s[r, c] = s[r, c] - s[r, k] * s[c, k]
                rows[c] = rows[c] - s[c, k] * rows[k]
                unit_rows[c] = unit_rows[c] - s[c, k] * unit_rows[k]
                for g in range(1, groups - b):
                    cols[c][g] = cols[c][g] - s[c, k] * cols[k][g]
        for g in range(1, groups - b):
            at = slice(r0 + 8 * g, r0 + 8 * g + 8)
            take = [cols[k][g] * rows[k] for k in range(8)]
            work[at, :] = work[at, :] - (
                ((take[0] + take[1]) + (take[2] + take[3]))
                + ((take[4] + take[5]) + (take[6] + take[7]))
            )
            take = [cols[k][g] * unit_rows[k] for k in range(8)]
            unit[at, :] = unit[at, :] - (
                ((take[0] + take[1]) + (take[2] + take[3]))
                + ((take[4] + take[5]) + (take[6] + take[7]))
            )
        for k in range(8):
            upper[r0 + k : r0 + k + 1, :] = rows[k][:1]
            lower_inv[r0 + k : r0 + k + 1, :] = unit_rows[k][:1]


def first_half(block, work, unit, upper, lower_inv, spread, outs):
    factor, inverse, below, rest = outs
    row = lax.broadcasted_iota(jnp.int32, (HB, HB), 0)
    col = lax.broadcasted_iota(jnp.int32, (HB, HB), 1)
    work[...] = block[0]
    unit[...] = jnp.where(row == col, 1.0, 0.0)
    half_factor(work, unit, upper, lower_inv, spread)
    factor[...] = jnp.where(row >= col, upper[...].T, 0.0)
    inverse[...] = lower_inv[...]
    strip = dot_nt(block[1], lower_inv[...])
    below[...] = strip
    rest[...] = block[2] - dot_nt(strip, strip)


def start_kernel(block, factor, inverse, below, rest, work, unit, upper, lower_inv, spread):
    first_half(block, work, unit, upper, lower_inv, spread, (factor, inverse, below, rest))


def next_kernel(
    side, turned, block, prior, cross, factor, inverse, below, rest, left, work, unit, upper, lower_inv, spread
):
    raw = jnp.concatenate(
        [
            jnp.concatenate([side[0], turned[1].T], axis=1),
            jnp.concatenate([side[1], side[2]], axis=1),
        ],
        axis=0,
    )
    solved = dot_nt(raw, prior[...])
    cross[...] = solved
    update = dot_nt(solved, solved)
    left[0] = block[0] - update[:HB, :HB]
    left[1] = block[1] - update[HB:, :HB]
    left[2] = block[2] - update[HB:, HB:]
    first_half(left, work, unit, upper, lower_inv, spread, (factor, inverse, below, rest))


def finish_kernel(
    factor, inverse, below, rest, whole_factor, whole_inverse, work, unit, upper, lower_inv, spread
):
    row = lax.broadcasted_iota(jnp.int32, (HB, HB), 0)
    col = lax.broadcasted_iota(jnp.int32, (HB, HB), 1)
    work[...] = rest[...]
    unit[...] = jnp.where(row == col, 1.0, 0.0)
    half_factor(work, unit, upper, lower_inv, spread)
    whole_factor[:HB, :HB] = factor[...]
    whole_factor[:HB, HB:] = jnp.zeros((HB, HB), jnp.float32)
    whole_factor[HB:, :HB] = below[...]
    whole_factor[HB:, HB:] = jnp.where(row >= col, upper[...].T, 0.0)
    whole_inverse[:HB, :HB] = inverse[...]
    whole_inverse[:HB, HB:] = jnp.zeros((HB, HB), jnp.float32)
    whole_inverse[HB:, :HB] = -dot_nn(lower_inv[...], dot_nn(below[...], inverse[...]))
    whole_inverse[HB:, HB:] = lower_inv[...]


def factor_call(fn, args, outs, extra=()):
    half = pltpu.VMEM((HB, HB), jnp.float32)
    return pl.pallas_call(
        fn,
        out_shape=[jax.ShapeDtypeStruct(s, jnp.float32) for s in outs],
        scratch_shapes=[
            *extra,
            half,
            half,
            half,
            half,
            pltpu.VMEM((64, HB), jnp.float32),
        ],
        compiler_params=pltpu.CompilerParams(vmem_limit_bytes=32 * 2**20),
        cost_estimate=pl.CostEstimate(flops=0, bytes_accessed=0, transcendentals=0),
    )(*args)


QUARTERS = [(HB, HB)] * 4


def split(x):
    high = x.astype(jnp.bfloat16)
    return high, (x - high.astype(jnp.float32)).astype(jnp.bfloat16)


def mul(a, b):
    return jnp.dot(a, b, preferred_element_type=jnp.float32)


def mul_nt(a, b):
    return lax.dot_general(a, b, (((1,), (1,)), ((), ())), preferred_element_type=jnp.float32)


def wide_left(x):
    high, low = split(x)
    return jnp.concatenate([high, high, low], axis=1)


def wide_right(x):
    high, low = split(x)
    return jnp.concatenate([high, low, high], axis=1)


def solve_both(first, second, first_inverse, cross, second_inverse):
    left = mul_nt(wide_left(first), first_inverse)
    right = mul_nt(wide_left(second - mul_nt(wide_left(left), cross)), second_inverse)
    return left, right


def in_order(middle, others):
    return jnp.concatenate([others[:1], middle[...], others[1:]], axis=0).reshape(-1, NB)


def update_kernel(n_row, n_col, step_of, count, first_block, col_parts, *refs):
    (place, matrix, noise, own, twin, here, there) = refs[:7]
    (first_factor, first_inverse, cross, second_factor, second_inverse) = refs[7:12]
    refs = refs[12:]
    if col_parts:
        raw_cols, (out, high, low) = refs[:col_parts], refs[col_parts : col_parts + 3]
        refs = refs[col_parts + 3 :]
    else:
        high, low, _, out = refs[:4]
        refs = refs[4:]
    tiles, rows_wide, edge, in_sem, out_sem = refs
    p, q = place[0], place[2]
    col_count = matrix.shape[1] // NB

    def rows_at(r):
        start = step_of(r) * NB
        return pl.ds(start if isinstance(start, int) else pl.multiple_of(start, NB), NB)

    def fetch(r):
        return pltpu.make_async_copy(matrix.at[rows_at(r), :], tiles.at[r], in_sem.at[r])

    def leave(r):
        return pltpu.make_async_copy(tiles.at[r], out.at[rows_at(r), :], out_sem.at[r])

    for r in range(count):
        fetch(r).start()
    inverses = (
        wide_right(first_inverse[...]),
        wide_right(cross[...]),
        wide_right(second_inverse[...]),
    )
    if col_parts:
        odd = place[1] == 1
        if col_parts == 2:
            mine, other = raw_cols[0][...], raw_cols[1][...]
        else:
            mine, other = in_order(*raw_cols[:2]), in_order(*raw_cols[2:])
        left, right = solve_both(
            jnp.where(odd, other, mine), jnp.where(odd, mine, other), *inverses
        )
        high[:NB], low[:NB] = split(left.T)
        high[NB:], low[NB:] = split(right.T)
    part = slice(first_block, first_block + count)
    by_columns = jnp.where(place[5] == 1, here[part], there[part])
    by_core = jnp.where(place[6] == 0, twin[...], own[...])
    first = jnp.where(place[3] == 1, own[...], twin[...])
    second = jnp.where(place[4] == 1, by_columns, by_core)
    left, right = solve_both(first.reshape(-1, NB), second.reshape(-1, NB), *inverses)
    edge[...] = jnp.where(q == 0, left, right).reshape(edge.shape)
    left_high, left_low = split(left)
    right_high, right_low = split(right)
    rows_wide[:, :NB] = left_high
    rows_wide[:, NB : 2 * NB] = right_high
    rows_wide[:, 2 * NB : 3 * NB] = left_low
    rows_wide[:, 3 * NB :] = right_low
    row = lax.broadcasted_iota(jnp.int32, (NB, NB), 0)
    col = lax.broadcasted_iota(jnp.int32, (NB, NB), 1)

    def one(r, _):
        here = pl.ds(pl.multiple_of(r * NB, NB), NB)
        i = step_of(r) * n_row + p
        active = jnp.minimum(lax.div(i - q + n_col, n_col), col_count)
        fetch(r).wait()
        for blocks in range(1, col_count + 1):

            @pl.when(active == blocks)
            def _():
                both = rows_wide[here, : 2 * NB]
                wide = jnp.concatenate([both, both, rows_wide[here, 2 * NB :]], axis=1)
                for c in range(blocks):
                    at = slice(c * NB, c * NB + NB)
                    tall = jnp.concatenate([high[:, at], low[:, at], high[:, at]], axis=0)
                    tiles[r, :, at] = tiles[r, :, at] - mul(wide, tall)

                @pl.when(i == (blocks - 1) * n_col + q)
                def _():
                    tiles[r, :, at] += jnp.where(row == col, noise[step_of(r)], 0.0)

        @pl.when((q < 2) & (i > q))
        def _():
            tiles[r, :, :NB] = jnp.where((q == 0) & (i == 1), cross[...], edge[r])

        @pl.when((q < 2) & (i == q))
        def _():
            tiles[r, :, :NB] = jnp.where(q == 0, first_factor[...], second_factor[...])

        leave(r).start()
        return 0

    lax.fori_loop(0, count, one, 0)
    for r in range(count):
        leave(r).wait()


def update(
    place, step_of, count, matrix, noise, rows, factored, n_row, n_col, first_block=0, cols=(), done=None
):
    cols_local = matrix.shape[1]
    whole = pl.BlockSpec(memory_space=pltpu.VMEM)
    anywhere = pl.BlockSpec(memory_space=pl.ANY)
    part = jax.ShapeDtypeStruct((2 * NB, cols_local), jnp.bfloat16)
    result = jax.ShapeDtypeStruct(matrix.shape, jnp.float32)
    extra = cols if done is None else (*done[1:], done[0])
    solved = count + (cols_local // NB if done is None else 0)
    flops = 2 * 3 * NB * NB * (solved * 3 * NB + count * cols_local)
    outs = pl.pallas_call(
        functools.partial(update_kernel, n_row, n_col, step_of, count, first_block, len(cols)),
        in_specs=[pl.BlockSpec(memory_space=pltpu.SMEM), anywhere]
        + [whole] * 10
        + ([whole] * len(cols) if done is None else [whole, whole, anywhere]),
        out_specs=[anywhere, whole, whole] if done is None else anywhere,
        out_shape=[result, part, part] if done is None else result,
        scratch_shapes=[
            pltpu.VMEM((count, NB, cols_local), jnp.float32),
            pltpu.VMEM((count * NB, 4 * NB), jnp.bfloat16),
            pltpu.VMEM((count, NB, NB), jnp.float32),
            pltpu.SemaphoreType.DMA((count,)),
            pltpu.SemaphoreType.DMA((count,)),
        ],
        input_output_aliases={} if done is None else {14: 0},
        compiler_params=pltpu.CompilerParams(vmem_limit_bytes=40 * 2**20),
        cost_estimate=pl.CostEstimate(
            flops=flops, bytes_accessed=count * NB * cols_local * 8, transcendentals=0
        ),
    )(place, matrix, noise, *rows, *factored, *extra)
    return outs if done is None else (outs, *done[1:])


def pick_kernel(cases, which, *refs):
    sources, out, sems = refs[:-2], refs[-2], refs[-1]
    for number, case in enumerate(cases):

        @pl.when(which[0] == number)
        def _():
            copies = [
                pltpu.make_async_copy(sources[k].at[at], out.at[b], sems.at[b])
                for b, (k, at) in enumerate(case)
            ]
            for copy in copies:
                copy.start()
            for copy in copies:
                copy.wait()


def pick(cases):
    sources, lists, which = [], [], jnp.int32(len(cases) - 1)
    for condition, case in cases:
        places = []
        for array, at in case:
            known = [k for k, x in enumerate(sources) if x is array]
            if not known:
                sources.append(array)
            places.append((known[0] if known else len(sources) - 1, at))
        lists.append(places)
    for number in reversed(range(len(cases) - 1)):
        which = jnp.where(cases[number][0], number, which)
    count = len(lists[0])
    return pl.pallas_call(
        functools.partial(pick_kernel, lists),
        in_specs=[pl.BlockSpec(memory_space=pltpu.SMEM)]
        + [pl.BlockSpec(memory_space=pl.ANY)] * len(sources),
        out_specs=pl.BlockSpec(memory_space=pltpu.VMEM),
        out_shape=jax.ShapeDtypeStruct((count, NB, NB), jnp.float32),
        scratch_shapes=[pltpu.SemaphoreType.DMA((count,))],
        cost_estimate=pl.CostEstimate(flops=0, bytes_accessed=0, transcendentals=0),
    )(which.astype(jnp.int32).reshape(1), *sources)


def start_factor(corner):
    return factor_call(start_kernel, [corner], QUARTERS)


def finish_factor(part, side, turned, next_corner, before_first=(), before_last=()):
    part = [after(part[0], *before_first), *part[1:]]
    first_factor, first_inverse = factor_call(finish_kernel, part, [(NB, NB)] * 2)
    cross, *part = factor_call(
        next_kernel,
        [side, turned, next_corner, first_inverse],
        [(NB, NB)] + QUARTERS,
        [pltpu.VMEM((3, HB, HB), jnp.float32)],
    )
    part = [after(part[0], *before_last), *part[1:]]
    second_factor, second_inverse = factor_call(finish_kernel, part, [(NB, NB)] * 2)
    return first_factor, first_inverse, cross, second_factor, second_inverse


def low_part(x):
    return jnp.stack([x[:HB, :HB], x[HB:, :HB], x[HB:, HB:]])


def after(x, *others):
    return lax.optimization_barrier((x, *others))[0]


def blocks_of(x):
    return x.reshape(-1, NB, NB)


def head_noise(noise):
    return jnp.where(jnp.arange(NB)[:, None] == jnp.arange(NB)[None, :], noise[:NB, None], 0.0)


def arrange(own, other, core):
    first = jnp.where(core == 0, own, other)
    second = jnp.where(core == 0, other, own)
    return first[0], first[1], second[0], second[1]


def body_general(kernel, noise):
    n_row = lax.axis_size("row")
    n_col = lax.axis_size("col")
    p = lax.axis_index("row")
    q = lax.axis_index("col")
    chunks = kernel.shape[0] // NB
    planes = n_col // 2
    plane = q // 2
    core = q % 2

    def twin(x):
        return lax.ppermute(x, "col", [(c, c ^ 1) for c in range(n_col)])

    mine = blocks_of(kernel[:, :NB])
    sent, other, got = [], [], None
    for s in range(chunks + planes - 1):
        now = mine[0] if s == 0 else got
        if 0 < s < chunks:
            now = jnp.where(plane == 0, mine[s], got)
        sent.append(now)
        other.append(twin(now))
        pairs = [
            (2 * z + c, 2 * z + 2 + c)
            for z in range(planes - 1)
            if 0 <= s - z < chunks
            for c in range(2)
        ]
        if pairs:
            got = lax.ppermute(now, "col", pairs)
    own = lax.dynamic_slice_in_dim(jnp.stack(sent), plane, chunks)
    other = lax.dynamic_slice_in_dim(jnp.stack(other), plane, chunks)

    block = own[0]
    block = low_part(jnp.where(p == core, block + head_noise(noise), block))
    swapped = lax.ppermute(block, "row", [(r, r ^ 1) for r in range(2)])
    even = p % 2 == 0
    strip = jnp.stack([jnp.where(even, block, swapped), jnp.where(even, swapped, block)])
    step = 2
    while step < n_row:
        more = lax.ppermute(strip, "row", [(r, r + step) for r in range(step)])
        strip = jnp.where(p >= step, more, strip)
        step *= 2
    corner, *rest = arrange(strip, twin(strip), core)
    factored = finish_factor(start_factor(corner), *rest)

    tops = lax.all_gather(kernel[:NB].T, "row")
    none = jnp.zeros_like(p)
    place = jnp.stack([p, none, q, 1 - core, none, none, core]).astype(jnp.int32)
    return update(
        place,
        lambda r: r,
        chunks,
        kernel,
        noise.reshape(-1, 1, NB),
        (own, other, own, own),
        factored,
        n_row,
        n_col,
        cols=(tops[0], tops[1]),
    )[0]


BOTH = ("row", "col")
N_COL = 8


def route(x, pairs):
    return lax.ppermute(x, BOTH, [(a[0] * N_COL + a[1], b[0] * N_COL + b[1]) for a, b in pairs])


def spread_inverses(factored, earlier, between, plane, core):
    _, first, cross, _, second = factored
    halves = (
        jnp.concatenate([low_part(first), jnp.stack([cross[:HB, :HB], cross[:HB, HB:]])]),
        jnp.concatenate([jnp.stack([cross[HB:, :HB], cross[HB:, HB:]]), low_part(second)]),
    )
    here = after(jnp.where(core == 0, halves[0], halves[1]), *earlier)
    z = route(here, [((r, c), (r, 4 + c)) for r in range(4) for c in (0, 1)])
    here = after(jnp.where(plane == 2, z, here), *between)
    z = route(here, [((r, k + c), (r, k + 2 + c)) for r in range(4) for k in (0, 4) for c in (0, 1)])
    here = jnp.where(plane % 2 == 1, z, here)
    other = route(here, TWINS)
    top = jnp.where(core == 0, here, other)
    low = jnp.where(core == 0, other, here)
    zero = jnp.zeros((HB, HB), jnp.float32)

    def square(a, b, c, d):
        return jnp.concatenate(
            [jnp.concatenate([a, b], axis=1), jnp.concatenate([c, d], axis=1)], axis=0
        )

    return (
        square(top[0], zero, top[1], top[2]),
        square(top[3], top[4], low[0], low[1]),
        square(low[2], zero, low[3], low[4]),
    )


TWINS = [((r, c), (r, c ^ 1)) for r in range(4) for c in range(N_COL)]


def body_four(kernel, noise):
    p = lax.axis_index("row")
    q = lax.axis_index("col")
    plane = q // 2
    core = q % 2
    home = core == p % 2
    low_line = p < 2
    n_cols = kernel.shape[1] // NB
    cut = (n_cols - 1) // 2
    early, late = slice(1, 1 + cut), slice(1 + cut, 1 + 2 * cut)

    strips = kernel.reshape(n_cols, 2, NB, -1)

    def even(part):
        return strips[part, 0, :, :NB]

    def odd(part):
        return strips[part, 1, :, :NB]

    blocks = blocks_of(kernel[:NB].T)
    middle = blocks[early]
    others = jnp.concatenate([blocks[:1], blocks[late]], axis=0)
    along_y = [((a, c), (a + 2, c)) for a in range(2) for c in range(N_COL)]
    along_x = [((a, c), (a ^ 1, c)) for a in range(4) for c in range(N_COL)]
    low, high = (0, 1), (2, 3)
    up = lambda z, lines: [((r, 2 * z + c), (r, 2 * z + 2 + c)) for r in lines for c in (0, 1)]
    lift = [((s, 4 + r), (r, 6 + s)) for r in low for s in (0, 1)]
    side = [((2 + s, r), (r, 4 + s)) for r in high for s in (0, 1)]
    corner = kernel[:NB, :NB]
    corner = low_part(jnp.where(p == core, corner + head_noise(noise), corner))

    got = route(corner, [((r, c), (r + 2, c)) for r in (0, 1) for c in (0, 1)])
    y1 = route(after(middle, got), along_y)
    h1 = route(jnp.where(plane == 0, even(early), middle), up(0, low) + lift)
    here = jnp.where(low_line, corner, got)
    lead_x = route(here, [((r, c), (r ^ 1, c)) for r in range(4) for c in (0, 1)])
    is_even = p % 2 == 0
    lead = jnp.stack([jnp.where(is_even, here, lead_x), jnp.where(is_even, lead_x, here)])
    lead_twin = route(lead, [((r, c), (r, c ^ 1)) for r in range(4) for c in (0, 1)])
    corner, *rest = arrange(lead, lead_twin, core)
    begun = start_factor(after(corner, h1))

    others = after(others, lead_x)
    y2 = route(others, along_y)
    mine1 = after(jnp.where(low_line, after(middle, lead_x), y1), begun[0])
    x1 = route(mine1, along_x)

    h2 = route(
        jnp.where(
            plane == 0,
            even(late),
            jnp.where(plane == 1, jnp.where(low_line, h1, mine1), others[1:]),
        ),
        up(0, low) + up(1, low) + side + lift,
    )
    homes = {0: (0, 4), 1: (1, 5), 2: (2, 6), 3: (3, 7)}
    down = [(at, (r, at[1] - 2)) for r, at in homes.items()]
    down_other = [(at, (r, (at[1] - 2) ^ 1)) for r, at in homes.items()]
    mine_down1 = route(mine1, down)
    risen = route(after(odd(slice(0, n_cols)), lead_x), up(0, high))
    factored = finish_factor(begun, *rest, before_last=(x1, h2, y2))
    cross = factored[2]
    mine2 = jnp.where(low_line, after(others, cross), y2)
    x2 = route(after(mine2, x1), along_x)
    mine_down2 = route(mine2, down)
    other_down1 = route(after(x1, cross), down_other)
    other_down2 = route(x2, down_other)
    h2 = after(h2, cross)
    h3 = route(
        jnp.where((plane == 1) & ~low_line, mine2[1:], h2), up(1, low) + side + up(2, low + high)
    )
    h4 = route(h3, up(2, low + high))
    inverses = spread_inverses(
        factored, (h2, risen, mine_down1), (x2, h3, mine_down2, other_down1), plane, core
    )
    factored = (factored[0], inverses[0], inverses[1], factored[3], after(inverses[2], h4))

    by_odd = (low_line & (plane == 2)) | (~low_line & (plane == 3))
    by_even = ~low_line & (plane == 1)

    def local(steps):
        return [(kernel, (pl.ds(NB * t, NB), pl.ds(0, NB))) for t in steps]

    def ordered(mid, rest, part):
        whole = [(rest, 0)] + [(mid, c) for c in range(cut)] + [(rest, 1 + c) for c in range(cut)]
        return whole[part]

    def simple(x, steps):
        return [(x, c) for c in steps]

    everything, start = slice(0, n_cols), slice(0, 1 + cut)
    second_cols = pick(
        [(is_even, ordered(x1, x2, everything)), (None, ordered(mine1, mine2, everything))]
    )
    col_homes = [(at, (at[0], at[1] ^ 1)) for at in (*homes.values(), (2, 2), (3, 3))]
    second_twin = route(second_cols, col_homes)
    clipped = [max(c - 1, 0) for c in range(1 + cut)]
    own_early = pick(
        [
            (plane == 0, local(range(0, 2 + 2 * cut, 2))),
            (by_even & is_even, ordered(mine1, mine2, start)),
            (by_even, ordered(x1, x2, start)),
            (plane == 1, simple(h1, clipped)),
            (plane == 2, simple(h2, clipped)),
            (None, simple(h3, clipped)),
        ]
    )
    own_late = pick(
        [
            (plane == 0, local(range(2 + 2 * cut, 2 * n_cols, 2))),
            (by_even & is_even, ordered(mine1, mine2, late)),
            (by_even, ordered(x1, x2, late)),
            (plane == 1, simple(h2, range(cut))),
            (plane == 2, simple(h3, range(cut))),
            (None, simple(h4, range(cut))),
        ]
    )

    def rows(own):
        return own, route(own, TWINS), second_cols, second_twin

    def place(by):
        flags = [p, p % 2, q, jnp.where(by, home, core == 0), by, home, core]
        return jnp.stack([x.astype(jnp.int32) for x in flags])

    noise_rows = noise.reshape(-1, 1, NB)
    rows_early, rows_late = rows(own_early), rows(own_late)
    args = (factored, 4, N_COL)
    done = update(
        place(by_even),
        lambda r: 2 * r,
        1 + cut,
        kernel,
        noise_rows,
        rows_early,
        *args,
        cols=(mine1, mine2, x1, x2),
    )
    mine_down1, mine_down2, other_down1, other_down2, _ = lax.optimization_barrier(
        (mine_down1, mine_down2, other_down1, other_down2, done[1])
    )
    own_odd = pick(
        [
            (plane == 0, local(range(1, 2 * n_cols, 2))),
            (by_odd & is_even, ordered(mine1, mine2, everything)),
            (by_odd, ordered(x1, x2, everything)),
            (by_even, simple(risen, range(n_cols))),
            (plane == 3, simple(h1, clipped) + simple(h2, range(cut))),
            (home, ordered(mine_down1, mine_down2, everything)),
            (None, ordered(other_down1, other_down2, everything)),
        ]
    )
    rows_odd = rows(own_odd)
    done = update(
        place(by_even),
        lambda r: 2 * (1 + cut + r),
        cut,
        kernel,
        noise_rows,
        rows_late,
        *args,
        first_block=1 + cut,
        done=done,
    )
    return update(
        place(by_odd), lambda r: 2 * r + 1, n_cols, kernel, noise_rows, rows_odd, *args, done=done
    )[0]


def body(kernel, noise):
    rows, cols = kernel.shape[0] // NB, kernel.shape[1] // NB
    mesh_of_four = lax.axis_size("row") == 4 and lax.axis_size("col") == N_COL
    if mesh_of_four and rows == 2 * cols and cols % 2 == 1 and cols > 2:
        return body_four(kernel, noise)
    return body_general(kernel, noise)


def solution(mesh):
    return jax.shard_map(
        body,
        mesh=mesh,
        in_specs=(P("row", "col"), P("row")),
        out_specs=P("row", "col"),
        check_vma=False,
    )
```

```python
import functools
import jax
import jax.numpy as jnp
from jax import lax
from jax.sharding import PartitionSpec as P
from jax.experimental import pallas as pl
from jax.experimental.pallas import tpu as pltpu

NB = 256
HB = 128
HIGHEST = lax.Precision.HIGHEST
GRANT = 8 * 2**20
UPDATE_GRANT = 44 * 2**20
PICK_GRANT = 44 * 2**20


def dot_nt(a, b):
    return lax.dot_general(
        a, b, (((1,), (1,)), ((), ())), precision=HIGHEST, preferred_element_type=jnp.float32
    )


def dot_nn(a, b):
    return jnp.dot(a, b, precision=HIGHEST, preferred_element_type=jnp.float32)


def half_factor(work, unit, upper, lower_inv, spread):
    groups = HB // 8
    for b in range(groups):
        r0 = 8 * b
        cols = []
        for c in range(8):
            col = [
                jnp.broadcast_to(work[8 * g : 8 * g + 8, r0 + c : r0 + c + 1], (8, HB))
                for g in range(b, groups)
            ]
            spread[8 * c : 8 * c + 8, :] = col[0]
            cols.append(col)
        s = {}
        for c in range(8):
            for r in range(c, 8):
                s[r, c] = jnp.broadcast_to(spread[8 * c + r : 8 * c + r + 1, :], (8, HB))
        rows = [jnp.broadcast_to(work[r0 + r : r0 + r + 1, :], (8, HB)) for r in range(8)]
        unit_rows = [jnp.broadcast_to(unit[r0 + r : r0 + r + 1, :], (8, HB)) for r in range(8)]
        for k in range(8):
            scale = lax.rsqrt(s[k, k])
            for r in range(k + 1, 8):
                s[r, k] = s[r, k] * scale
            rows[k] = rows[k] * scale
            unit_rows[k] = unit_rows[k] * scale
            for g in range(1, groups - b):
                cols[k][g] = cols[k][g] * scale
            for c in range(k + 1, 8):
                for r in range(c, 8):
                    s[r, c] = s[r, c] - s[r, k] * s[c, k]
                rows[c] = rows[c] - s[c, k] * rows[k]
                unit_rows[c] = unit_rows[c] - s[c, k] * unit_rows[k]
                for g in range(1, groups - b):
                    cols[c][g] = cols[c][g] - s[c, k] * cols[k][g]
        for g in range(1, groups - b):
            at = slice(r0 + 8 * g, r0 + 8 * g + 8)
            take = [cols[k][g] * rows[k] for k in range(8)]
            work[at, :] = work[at, :] - (
                ((take[0] + take[1]) + (take[2] + take[3]))
                + ((take[4] + take[5]) + (take[6] + take[7]))
            )
            take = [cols[k][g] * unit_rows[k] for k in range(8)]
            unit[at, :] = unit[at, :] - (
                ((take[0] + take[1]) + (take[2] + take[3]))
                + ((take[4] + take[5]) + (take[6] + take[7]))
            )
        for k in range(8):
            upper[r0 + k : r0 + k + 1, :] = rows[k][:1]
            lower_inv[r0 + k : r0 + k + 1, :] = unit_rows[k][:1]


def first_half(block, work, unit, upper, lower_inv, spread, outs):
    factor, inverse, below, rest = outs
    row = lax.broadcasted_iota(jnp.int32, (HB, HB), 0)
    col = lax.broadcasted_iota(jnp.int32, (HB, HB), 1)
    work[...] = block[0]
    unit[...] = jnp.where(row == col, 1.0, 0.0)
    half_factor(work, unit, upper, lower_inv, spread)
    factor[...] = jnp.where(row >= col, upper[...].T, 0.0)
    inverse[...] = lower_inv[...]
    strip = dot_nt(block[1], lower_inv[...])
    below[...] = strip
    rest[...] = block[2] - dot_nt(strip, strip)


def start_kernel(block, factor, inverse, below, rest, work, unit, upper, lower_inv, spread):
    first_half(block, work, unit, upper, lower_inv, spread, (factor, inverse, below, rest))


def next_kernel(
    side, turned, block, prior, cross, factor, inverse, below, rest, left, work, unit, upper, lower_inv, spread
):
    raw = jnp.concatenate(
        [
            jnp.concatenate([side[0], turned[1].T], axis=1),
            jnp.concatenate([side[1], side[2]], axis=1),
        ],
        axis=0,
    )
    solved = dot_nt(raw, prior[...])
    cross[...] = solved
    update = dot_nt(solved, solved)
    left[0] = block[0] - update[:HB, :HB]
    left[1] = block[1] - update[HB:, :HB]
    left[2] = block[2] - update[HB:, HB:]
    first_half(left, work, unit, upper, lower_inv, spread, (factor, inverse, below, rest))


def finish_kernel(
    factor, inverse, below, rest, whole_factor, whole_inverse, work, unit, upper, lower_inv, spread
):
    row = lax.broadcasted_iota(jnp.int32, (HB, HB), 0)
    col = lax.broadcasted_iota(jnp.int32, (HB, HB), 1)
    work[...] = rest[...]
    unit[...] = jnp.where(row == col, 1.0, 0.0)
    half_factor(work, unit, upper, lower_inv, spread)
    whole_factor[:HB, :HB] = factor[...]
    whole_factor[:HB, HB:] = jnp.zeros((HB, HB), jnp.float32)
    whole_factor[HB:, :HB] = below[...]
    whole_factor[HB:, HB:] = jnp.where(row >= col, upper[...].T, 0.0)
    whole_inverse[:HB, :HB] = inverse[...]
    whole_inverse[:HB, HB:] = jnp.zeros((HB, HB), jnp.float32)
    whole_inverse[HB:, :HB] = -dot_nn(lower_inv[...], dot_nn(below[...], inverse[...]))
    whole_inverse[HB:, HB:] = lower_inv[...]


def factor_call(fn, args, outs, extra=(), flops=0):
    half = pltpu.VMEM((HB, HB), jnp.float32)
    return pl.pallas_call(
        fn,
        out_shape=[jax.ShapeDtypeStruct(s, jnp.float32) for s in outs],
        scratch_shapes=[
            *extra,
            half,
            half,
            half,
            half,
            pltpu.VMEM((64, HB), jnp.float32),
        ],
        compiler_params=pltpu.CompilerParams(vmem_limit_bytes=GRANT),
        cost_estimate=pl.CostEstimate(flops=flops, bytes_accessed=0, transcendentals=0),
    )(*args)


QUARTERS = [(HB, HB)] * 4


def split(x):
    high = x.astype(jnp.bfloat16)
    return high, (x - high.astype(jnp.float32)).astype(jnp.bfloat16)


def mul(a, b):
    return jnp.dot(a, b, preferred_element_type=jnp.float32)


def mul_nt(a, b):
    return lax.dot_general(a, b, (((1,), (1,)), ((), ())), preferred_element_type=jnp.float32)


def wide_left(x):
    high, low = split(x)
    return jnp.concatenate([high, high, low], axis=1)


def wide_right(x):
    high, low = split(x)
    return jnp.concatenate([high, low, high], axis=1)


def solve_both(first, second, first_inverse, cross, second_inverse):
    left = mul_nt(wide_left(first), first_inverse)
    right = mul_nt(wide_left(second - mul_nt(wide_left(left), cross)), second_inverse)
    return left, right


def in_order(middle, others):
    return jnp.concatenate([others[:1], middle[...], others[1:]], axis=0).reshape(-1, NB)


def update_kernel(n_row, n_col, step_of, count, first_block, col_parts, *refs):
    (place, matrix, noise, own, twin, here, there) = refs[:7]
    (first_factor, first_inverse, cross, second_factor, second_inverse) = refs[7:12]
    refs = refs[12:]
    if col_parts:
        raw_cols, (out, high, low) = refs[:col_parts], refs[col_parts : col_parts + 3]
        refs = refs[col_parts + 3 :]
    else:
        high, low, _, out = refs[:4]
        refs = refs[4:]
    tiles, rows_wide, edge, in_sem, out_sem = refs
    p, q = place[0], place[2]
    col_count = matrix.shape[1] // NB

    def rows_at(r):
        start = step_of(r) * NB
        return pl.ds(start if isinstance(start, int) else pl.multiple_of(start, NB), NB)

    def fetch(r):
        return pltpu.make_async_copy(matrix.at[rows_at(r), :], tiles.at[r], in_sem.at[r])

    def leave(r):
        return pltpu.make_async_copy(tiles.at[r], out.at[rows_at(r), :], out_sem.at[r])

    for r in range(count):
        fetch(r).start()
    inverses = (
        wide_right(first_inverse[...]),
        wide_right(cross[...]),
        wide_right(second_inverse[...]),
    )
    if col_parts:
        odd = place[1] == 1
        if col_parts == 2:
            mine, other = raw_cols[0][...], raw_cols[1][...]
        else:
            mine, other = in_order(*raw_cols[:2]), in_order(*raw_cols[2:])
        left, right = solve_both(
            jnp.where(odd, other, mine), jnp.where(odd, mine, other), *inverses
        )
        high[:NB], low[:NB] = split(left.T)
        high[NB:], low[NB:] = split(right.T)
    part = slice(first_block, first_block + count)
    by_columns = jnp.where(place[5] == 1, here[part], there[part])
    by_core = jnp.where(place[6] == 0, twin[...], own[...])
    first = jnp.where(place[3] == 1, own[...], twin[...])
    second = jnp.where(place[4] == 1, by_columns, by_core)
    left, right = solve_both(first.reshape(-1, NB), second.reshape(-1, NB), *inverses)
    edge[...] = jnp.where(q == 0, left, right).reshape(edge.shape)
    left_high, left_low = split(left)
    right_high, right_low = split(right)
    rows_wide[:, :NB] = left_high
    rows_wide[:, NB : 2 * NB] = right_high
    rows_wide[:, 2 * NB : 3 * NB] = left_low
    rows_wide[:, 3 * NB :] = right_low
    row = lax.broadcasted_iota(jnp.int32, (NB, NB), 0)
    col = lax.broadcasted_iota(jnp.int32, (NB, NB), 1)

    def one(r, _):
        here = pl.ds(pl.multiple_of(r * NB, NB), NB)
        i = step_of(r) * n_row + p
        active = jnp.minimum(lax.div(i - q + n_col, n_col), col_count)
        fetch(r).wait()
        for blocks in range(1, col_count + 1):

            @pl.when(active == blocks)
            def _():
                both = rows_wide[here, : 2 * NB]
                wide = jnp.concatenate([both, both, rows_wide[here, 2 * NB :]], axis=1)
                for c in range(blocks):
                    at = slice(c * NB, c * NB + NB)
                    tall = jnp.concatenate([high[:, at], low[:, at], high[:, at]], axis=0)
                    tiles[r, :, at] = tiles[r, :, at] - mul(wide, tall)

                @pl.when(i == (blocks - 1) * n_col + q)
                def _():
                    tiles[r, :, at] += jnp.where(row == col, noise[step_of(r)], 0.0)

        @pl.when((q < 2) & (i > q))
        def _():
            tiles[r, :, :NB] = jnp.where((q == 0) & (i == 1), cross[...], edge[r])

        @pl.when((q < 2) & (i == q))
        def _():
            tiles[r, :, :NB] = jnp.where(q == 0, first_factor[...], second_factor[...])

        leave(r).start()
        return 0

    lax.fori_loop(0, count, one, 0)
    for r in range(count):
        leave(r).wait()


def update(
    place, step_of, count, matrix, noise, rows, factored, n_row, n_col, first_block=0, cols=(), done=None
):
    cols_local = matrix.shape[1]
    whole = pl.BlockSpec(memory_space=pltpu.VMEM)
    anywhere = pl.BlockSpec(memory_space=pl.ANY)
    part = jax.ShapeDtypeStruct((2 * NB, cols_local), jnp.bfloat16)
    result = jax.ShapeDtypeStruct(matrix.shape, jnp.float32)
    extra = cols if done is None else (*done[1:], done[0])
    solved = count + (cols_local // NB if done is None else 0)
    flops = 2 * 3 * NB * NB * (solved * 3 * NB + count * cols_local)
    outs = pl.pallas_call(
        functools.partial(update_kernel, n_row, n_col, step_of, count, first_block, len(cols)),
        in_specs=[pl.BlockSpec(memory_space=pltpu.SMEM), anywhere]
        + [whole] * 10
        + ([whole] * len(cols) if done is None else [whole, whole, anywhere]),
        out_specs=[anywhere, whole, whole] if done is None else anywhere,
        out_shape=[result, part, part] if done is None else result,
        scratch_shapes=[
            pltpu.VMEM((count, NB, cols_local), jnp.float32),
            pltpu.VMEM((count * NB, 4 * NB), jnp.bfloat16),
            pltpu.VMEM((count, NB, NB), jnp.float32),
            pltpu.SemaphoreType.DMA((count,)),
            pltpu.SemaphoreType.DMA((count,)),
        ],
        input_output_aliases={} if done is None else {14: 0},
        compiler_params=pltpu.CompilerParams(vmem_limit_bytes=UPDATE_GRANT),
        cost_estimate=pl.CostEstimate(
            flops=flops, bytes_accessed=count * NB * cols_local * 8, transcendentals=0
        ),
    )(place, matrix, noise, *rows, *factored, *extra)
    return outs if done is None else (outs, *done[1:])


def pick_kernel(cases, which, *refs):
    sources, out, sems = refs[:-2], refs[-2], refs[-1]
    for number, case in enumerate(cases):

        @pl.when(which[0] == number)
        def _():
            copies = [
                pltpu.make_async_copy(sources[k].at[at], out.at[b], sems.at[b])
                for b, (k, at) in enumerate(case)
            ]
            for copy in copies:
                copy.start()
            for copy in copies:
                copy.wait()


def pick(cases):
    sources, lists, which = [], [], jnp.int32(len(cases) - 1)
    for condition, case in cases:
        places = []
        for array, at in case:
            known = [k for k, x in enumerate(sources) if x is array]
            if not known:
                sources.append(array)
            places.append((known[0] if known else len(sources) - 1, at))
        lists.append(places)
    for number in reversed(range(len(cases) - 1)):
        which = jnp.where(cases[number][0], number, which)
    count = len(lists[0])
    return pl.pallas_call(
        functools.partial(pick_kernel, lists),
        in_specs=[pl.BlockSpec(memory_space=pltpu.SMEM)]
        + [pl.BlockSpec(memory_space=pl.ANY)] * len(sources),
        out_specs=pl.BlockSpec(memory_space=pltpu.VMEM),
        out_shape=jax.ShapeDtypeStruct((count, NB, NB), jnp.float32),
        scratch_shapes=[pltpu.SemaphoreType.DMA((count,))],
        compiler_params=pltpu.CompilerParams(vmem_limit_bytes=PICK_GRANT),
        cost_estimate=pl.CostEstimate(flops=0, bytes_accessed=0, transcendentals=0),
    )(which.astype(jnp.int32).reshape(1), *sources)


def start_factor(corner):
    return factor_call(start_kernel, [corner], QUARTERS)


def finish_factor(
    part, side, turned, next_corner, before_first=(), before_next=(), before_last=()
):
    part = [after(part[0], *before_first), *part[1:]]
    first_factor, first_inverse = factor_call(finish_kernel, part, [(NB, NB)] * 2)
    cross, *part = factor_call(
        next_kernel,
        [after(side, *before_next), turned, next_corner, first_inverse],
        [(NB, NB)] + QUARTERS,
        [pltpu.VMEM((3, HB, HB), jnp.float32)],
    )
    part = [after(part[0], *before_last), *part[1:]]
    second_factor, second_inverse = factor_call(
        finish_kernel, part, [(NB, NB)] * 2, flops=5 * 10**9
    )
    return first_factor, first_inverse, cross, second_factor, second_inverse


def low_part(x):
    return jnp.stack([x[:HB, :HB], x[HB:, :HB], x[HB:, HB:]])


def after(x, *others):
    return lax.optimization_barrier((x, *others))[0]


def blocks_of(x):
    return x.reshape(-1, NB, NB)


def head_noise(noise):
    return jnp.where(jnp.arange(NB)[:, None] == jnp.arange(NB)[None, :], noise[:NB, None], 0.0)


def arrange(own, other, core):
    first = jnp.where(core == 0, own, other)
    second = jnp.where(core == 0, other, own)
    return first[0], first[1], second[0], second[1]


def body_general(kernel, noise):
    n_row = lax.axis_size("row")
    n_col = lax.axis_size("col")
    p = lax.axis_index("row")
    q = lax.axis_index("col")
    chunks = kernel.shape[0] // NB
    planes = n_col // 2
    plane = q // 2
    core = q % 2

    def twin(x):
        return lax.ppermute(x, "col", [(c, c ^ 1) for c in range(n_col)])

    mine = blocks_of(kernel[:, :NB])
    sent, other, got = [], [], None
    for s in range(chunks + planes - 1):
        now = mine[0] if s == 0 else got
        if 0 < s < chunks:
            now = jnp.where(plane == 0, mine[s], got)
        sent.append(now)
        other.append(twin(now))
        pairs = [
            (2 * z + c, 2 * z + 2 + c)
            for z in range(planes - 1)
            if 0 <= s - z < chunks
            for c in range(2)
        ]
        if pairs:
            got = lax.ppermute(now, "col", pairs)
    own = lax.dynamic_slice_in_dim(jnp.stack(sent), plane, chunks)
    other = lax.dynamic_slice_in_dim(jnp.stack(other), plane, chunks)

    block = own[0]
    block = low_part(jnp.where(p == core, block + head_noise(noise), block))
    swapped = lax.ppermute(block, "row", [(r, r ^ 1) for r in range(2)])
    even = p % 2 == 0
    strip = jnp.stack([jnp.where(even, block, swapped), jnp.where(even, swapped, block)])
    step = 2
    while step < n_row:
        more = lax.ppermute(strip, "row", [(r, r + step) for r in range(step)])
        strip = jnp.where(p >= step, more, strip)
        step *= 2
    corner, *rest = arrange(strip, twin(strip), core)
    factored = finish_factor(start_factor(corner), *rest)

    tops = lax.all_gather(kernel[:NB].T, "row")
    none = jnp.zeros_like(p)
    place = jnp.stack([p, none, q, 1 - core, none, none, core]).astype(jnp.int32)
    return update(
        place,
        lambda r: r,
        chunks,
        kernel,
        noise.reshape(-1, 1, NB),
        (own, other, own, own),
        factored,
        n_row,
        n_col,
        cols=(tops[0], tops[1]),
    )[0]


BOTH = ("row", "col")
N_COL = 8


def route(x, pairs):
    return lax.ppermute(x, BOTH, [(a[0] * N_COL + a[1], b[0] * N_COL + b[1]) for a, b in pairs])


def spread_inverses(factored, earlier, between, plane, core):
    _, first, cross, _, second = factored
    halves = (
        jnp.concatenate([low_part(first), jnp.stack([cross[:HB, :HB], cross[:HB, HB:]])]),
        jnp.concatenate([jnp.stack([cross[HB:, :HB], cross[HB:, HB:]]), low_part(second)]),
    )
    here = after(jnp.where(core == 0, halves[0], halves[1]), *earlier)
    z = route(here, [((r, c), (r, 4 + c)) for r in range(4) for c in (0, 1)])
    here = after(jnp.where(plane == 2, z, here), *between)
    z = route(here, [((r, k + c), (r, k + 2 + c)) for r in range(4) for k in (0, 4) for c in (0, 1)])
    here = jnp.where(plane % 2 == 1, z, here)
    other = route(here, TWINS)
    top = jnp.where(core == 0, here, other)
    low = jnp.where(core == 0, other, here)
    zero = jnp.zeros((HB, HB), jnp.float32)

    def square(a, b, c, d):
        return jnp.concatenate(
            [jnp.concatenate([a, b], axis=1), jnp.concatenate([c, d], axis=1)], axis=0
        )

    return (
        square(top[0], zero, top[1], top[2]),
        square(top[3], top[4], low[0], low[1]),
        square(low[2], zero, low[3], low[4]),
    ), z


TWINS = [((r, c), (r, c ^ 1)) for r in range(4) for c in range(N_COL)]


def body_four(kernel, noise):
    p = lax.axis_index("row")
    q = lax.axis_index("col")
    plane = q // 2
    core = q % 2
    home = core == p % 2
    low_line = p < 2
    n_cols = kernel.shape[1] // NB
    cut = (n_cols - 1) // 2
    early, late = slice(1, 1 + cut), slice(1 + cut, 1 + 2 * cut)

    strips = kernel.reshape(n_cols, 2, NB, -1)

    def even(part):
        return strips[part, 0, :, :NB]

    def odd(part):
        return strips[part, 1, :, :NB]

    blocks = blocks_of(kernel[:NB].T)
    middle = blocks[early]
    others = jnp.concatenate([blocks[:1], blocks[late]], axis=0)
    along_y = [((a, c), (a + 2, c)) for a in range(2) for c in range(N_COL)]
    along_x = [((a, c), (a ^ 1, c)) for a in range(4) for c in range(N_COL)]
    low, high = (0, 1), (2, 3)
    up = lambda z, lines: [((r, 2 * z + c), (r, 2 * z + 2 + c)) for r in lines for c in (0, 1)]
    lift = [((s, 4 + r), (r, 6 + s)) for r in low for s in (0, 1)]
    side = [((2 + s, r), (r, 4 + s)) for r in high for s in (0, 1)]
    corner = kernel[:NB, :NB]
    corner = low_part(jnp.where(p == core, corner + head_noise(noise), corner))

    got = route(corner, [((r, c), (r + 2, c)) for r in (0, 1) for c in (0, 1)])
    y1 = route(middle, along_y)
    h1 = route(jnp.where(plane == 0, even(early), middle), up(0, low) + lift)
    here = jnp.where(low_line, corner, got)
    lead_x = route(here, [((r, c), (r ^ 1, c)) for r in range(4) for c in (0, 1)])
    is_even = p % 2 == 0
    lead = jnp.stack([jnp.where(is_even, here, lead_x), jnp.where(is_even, lead_x, here)])
    lead_twin = route(lead, [((r, c), (r, c ^ 1)) for r in range(4) for c in (0, 1)])
    corner, *rest = arrange(lead, lead_twin, core)
    begun = start_factor(corner)

    others = after(others, lead_twin)
    y2 = route(others, along_y)
    mine1 = jnp.where(low_line, after(middle, begun[0]), after(y1, begun[0]))
    x1 = route(mine1, along_x)

    h2 = route(
        jnp.where(
            plane == 0,
            even(late),
            jnp.where(plane == 1, jnp.where(low_line, h1, mine1), others[1:]),
        ),
        up(0, low) + up(1, low) + side + lift,
    )
    homes = {0: (0, 4), 1: (1, 5), 2: (2, 6), 3: (3, 7)}
    down = [(at, (r, at[1] - 2)) for r, at in homes.items()]
    down_other = [(at, (r, (at[1] - 2) ^ 1)) for r, at in homes.items()]
    mine_down1 = route(mine1, down)
    risen = route(after(odd(slice(0, n_cols)), lead_twin), up(0, high))
    mine2 = jnp.where(low_line, others, y2)
    x2 = route(after(mine2, x1), along_x)
    h3 = route(
        jnp.where((plane == 1) & ~low_line, mine2[1:], h2), up(1, low) + side + up(2, low + high)
    )
    factored = finish_factor(
        begun, *rest, before_first=(h1,), before_next=(y2, risen), before_last=(x1, h2, x2)
    )
    mine_down2 = route(after(mine2, factored[2]), down)
    other_down1 = route(after(x1, factored[2]), down_other)
    other_down2 = route(x2, down_other)
    h4 = route(after(h3, factored[2]), up(2, low + high))
    inverses, spread = spread_inverses(
        factored, (h3, mine_down1), (mine_down2, other_down1, h4), plane, core
    )
    factored = (factored[0], inverses[0], inverses[1], factored[3], inverses[2])

    by_odd = (low_line & (plane == 2)) | (~low_line & (plane == 3))
    by_even = ~low_line & (plane == 1)

    def local(steps):
        return [(kernel, (pl.ds(NB * t, NB), pl.ds(0, NB))) for t in steps]

    def ordered(mid, rest, part):
        whole = [(rest, 0)] + [(mid, c) for c in range(cut)] + [(rest, 1 + c) for c in range(cut)]
        return whole[part]

    def simple(x, steps):
        return [(x, c) for c in steps]

    everything, start = slice(0, n_cols), slice(0, 1 + cut)
    second_cols = pick(
        [(is_even, ordered(x1, x2, everything)), (None, ordered(mine1, mine2, everything))]
    )
    col_homes = [(at, (at[0], at[1] ^ 1)) for at in (*homes.values(), (2, 2), (3, 3))]
    second_twin = route(second_cols, col_homes)
    clipped = [max(c - 1, 0) for c in range(1 + cut)]
    def rows(own):
        return own, route(own, TWINS), second_cols, second_twin

    def place(by):
        flags = [p, p % 2, q, jnp.where(by, home, core == 0), by, home, core]
        return jnp.stack([x.astype(jnp.int32) for x in flags])

    noise_rows = noise.reshape(-1, 1, NB)
    own_odd = pick(
        [
            (plane == 0, local(range(1, 2 * n_cols, 2))),
            (by_odd & is_even, ordered(mine1, mine2, everything)),
            (by_odd, ordered(x1, x2, everything)),
            (by_even, simple(risen, range(n_cols))),
            (plane == 3, simple(h1, clipped) + simple(h2, range(cut))),
            (home, ordered(mine_down1, mine_down2, everything)),
            (None, ordered(other_down1, other_down2, everything)),
        ]
    )
    own_early = pick(
        [
            (plane == 0, local(range(0, 2 + 2 * cut, 2))),
            (by_even & is_even, ordered(mine1, mine2, start)),
            (by_even, ordered(x1, x2, start)),
            (plane == 1, simple(h1, clipped)),
            (plane == 2, simple(h2, clipped)),
            (None, simple(h3, clipped)),
        ]
    )
    rows_early = rows(own_early)
    args = (factored, 4, N_COL)
    done = update(
        place(by_odd),
        lambda r: 2 * r + 1,
        n_cols,
        kernel,
        noise_rows,
        rows(own_odd),
        *args,
        cols=(mine1, mine2, x1, x2),
    )
    h4 = after(h4, done[1])
    own_late = pick(
        [
            (plane == 0, local(range(2 + 2 * cut, 2 * n_cols, 2))),
            (by_even & is_even, ordered(mine1, mine2, late)),
            (by_even, ordered(x1, x2, late)),
            (plane == 1, simple(h2, range(cut))),
            (plane == 2, simple(h3, range(cut))),
            (None, simple(h4, range(cut))),
        ]
    )
    rows_late = rows(own_late)
    done = update(
        place(by_even), lambda r: 2 * r, 1 + cut, kernel, noise_rows, rows_early, *args, done=done
    )
    return update(
        place(by_even),
        lambda r: 2 * (1 + cut + r),
        cut,
        kernel,
        noise_rows,
        rows_late,
        *args,
        first_block=1 + cut,
        done=done,
    )[0]


def body(kernel, noise):
    rows, cols = kernel.shape[0] // NB, kernel.shape[1] // NB
    mesh_of_four = lax.axis_size("row") == 4 and lax.axis_size("col") == N_COL
    if mesh_of_four and rows == 2 * cols and cols % 2 == 1 and cols > 2:
        return body_four(kernel, noise)
    return body_general(kernel, noise)


def solution(mesh):
    return jax.shard_map(
        body,
        mesh=mesh,
        in_specs=(P("row", "col"), P("row")),
        out_specs=P("row", "col"),
        check_vma=False,
    )
```
